512 devices in a mesh: dp: 16 (over z), expert: 32 (over y, x, core).
Axes of the slice: x: 4, y: 4, z: 16, core: 2. Of those that a mesh axis runs over, the one named last changes fastest.
Arguments:
- out_grad: bfloat16 [131072, 1440], P(('dp', 'expert')), may hold values from -6 to 6
- gates: float32 [131072], P(('dp', 'expert')), may hold values from 0.05 to 0.6
- expert_ids: int32 [131072], P(('dp', 'expert')), may hold values from 0 to 31, as said below
- saved_gate: bfloat16 [163840, 1440], P(('dp', 'expert')), may hold values from -6 to 6
- saved_up: bfloat16 [163840, 1440], P(('dp', 'expert')), may hold values from -6 to 6
- w_gate: bfloat16 [32, 1440, 1440], P('expert', 'dp'), may hold values from -0.15625 to 0.15625
- w_up: bfloat16 [32, 1440, 1440], P('expert', 'dp'), may hold values from -0.15625 to 0.15625
- w_down: bfloat16 [32, 1440, 1440], P('expert', 'dp'), may hold values from -0.15625 to 0.15625
Outputs:
- d_tokens: bfloat16 [131072, 1440], P(('dp', 'expert'))
- grad_down: float32 [32, 1440, 1440], P('expert', 'dp')
The draws below stay inside these ranges and needn't reach their ends.
Inputs may be any that keep to these rules, and one draw needn't show every extreme that they name: `expert_ids`: among the tokens of one device, no expert is named by more than 10 tokens; in every draw one expert is named by exactly 10 tokens of every device.
All inputs are finite; a program needn't handle non-finite values.
Results may differ from the reference program's by a relative error of at most 0.019.
Values may be sent and summed in bfloat16 or wider, within the bound.
No kernel may reach another device: no remote copies, remote signals or barrier semaphores. Data moves between devices by JAX's collectives and lax.ppermute only.
A program may use at most 128 MiB of HBM per device.

```python
import math
import jax
import jax.numpy as jnp
from jax import lax

DW = 1440
FW = 1440
TOK_DEV = 256
EXPERTS = 32
CAP = 10
TOKENS = 131072
DEVICES = 512


def draw_expert_ids(key, part):
    key = jax.random.fold_in(key, 11)
    favour_key, heavy_key, block_key = jax.random.split(key, 3)
    slot_count = EXPERTS * CAP
    owner = jnp.arange(slot_count, dtype=jnp.int32) // CAP
    favour = jax.random.randint(favour_key, (EXPERTS,), 0, slot_count, dtype=jnp.int32)
    heavy = jax.random.randint(heavy_key, (), 0, EXPERTS, dtype=jnp.int32)
    blocks = TOKENS // TOK_DEV

    def one_block(this_key):
        pick_key, order_key = jax.random.split(this_key)
        shuffled = jax.random.permutation(pick_key, slot_count).astype(jnp.int32)
        priority = jnp.where(owner == heavy, -1, shuffled + favour[owner])
        chosen = jnp.argsort(priority, stable=True)[:TOK_DEV]
        picked = owner[chosen]
        return picked[jax.random.permutation(order_key, TOK_DEV)]
    result = jax.vmap(one_block)(jax.random.split(block_key, blocks))
    return result.reshape(TOKENS).astype(jnp.int32)


def shard_levels(stream_key, dims, cuts, smallest, high):
    loudness = 1.0
    for axis_at, blocks in cuts:
        draws = jax.random.uniform(jax.random.fold_in(jax.random.fold_in(stream_key, 6), axis_at), (blocks,), jnp.float32, smallest / len(cuts), high / len(cuts))
        loudness = loudness * jnp.repeat(jnp.exp(draws), dims[axis_at] // blocks).reshape((-1,) + (1,) * (len(dims) - 1 - axis_at))
    return loudness


def gaussian(key, extent, scale, limit, cuts=(), kind=jnp.bfloat16):
    gain = shard_levels(key, extent, cuts, -0.22, 0.18) if cuts else 1.0
    drawn = jax.random.normal(key, extent, jnp.float32) * scale * gain
    return jnp.minimum(jnp.maximum(drawn, -limit), limit).astype(kind)


def setup_inputs(seed: int = 0) -> dict:
    arg_keys = jax.random.split(jax.random.key(seed), 9)
    return {
        "out_grad": gaussian(arg_keys[0], (TOKENS, DW), 1.0, 6.0, ((0, 512),)),
        "gates": jnp.clip(jnp.exp(math.log(0.6) - 2.4849067 * jax.random.uniform(arg_keys[1], (TOKENS,), jnp.float32) ** shard_levels(arg_keys[1], (TOKENS,), ((0, 512),), -0.2, 0.2)), 0.05, 0.6),
        "expert_ids": draw_expert_ids(jax.random.fold_in(arg_keys[8], 71), 0),
        "saved_gate": gaussian(arg_keys[3], (DEVICES * EXPERTS * CAP, FW), 1.5, 6.0, ((0, 512),)),
        "saved_up": gaussian(arg_keys[4], (DEVICES * EXPERTS * CAP, FW), 1.0, 6.0, ((0, 512),)),
        "w_gate": gaussian(arg_keys[5], (EXPERTS, DW, FW), DW ** -0.5, 0.15625, ((0, 32), (1, 16))),
        "w_up": gaussian(arg_keys[6], (EXPERTS, DW, FW), DW ** -0.5, 0.15625, ((0, 32), (1, 16))),
        "w_down": gaussian(arg_keys[7], (EXPERTS, FW, DW), DW ** -0.5, 0.15625, ((0, 32), (1, 16))),
    }


def reference(out_grad, gates, expert_ids, saved_gate, saved_up, w_gate, w_up, w_down):
    n_exp = EXPERTS
    blocks = TOKENS // TOK_DEV
    n_groups = blocks // n_exp
    ids = expert_ids.reshape(blocks, TOK_DEV)
    onehot = (ids[:, :, None] == jnp.arange(n_exp, dtype=jnp.int32)[None, None, :]).astype(jnp.int32)
    earlier = jnp.cumsum(onehot, axis=1) - onehot
    rank = jnp.sum(earlier * onehot, axis=2).astype(jnp.int32)
    device = jnp.arange(blocks, dtype=jnp.int32)[:, None]
    group = device // n_exp
    source = device % n_exp
    slot = (((group * n_exp + ids) * n_exp + source) * CAP + rank).reshape(TOKENS).astype(jnp.int32)
    scaled = (gates[:, None] * out_grad.astype(jnp.float32)).astype(jnp.bfloat16)
    total_slots = blocks * n_exp * CAP
    slot_rows = jnp.zeros((total_slots, DW), jnp.bfloat16).at[slot].set(scaled)
    per_slots = n_exp * CAP
    slot_rows = jnp.moveaxis(slot_rows.reshape(n_groups, n_exp, per_slots, DW), 1, 0)
    gate_rows = jnp.moveaxis(saved_gate.reshape(n_groups, n_exp, per_slots, FW), 1, 0)
    up_rows = jnp.moveaxis(saved_up.reshape(n_groups, n_exp, per_slots, FW), 1, 0)

    def one_expert(items):
        arrived, gate_pre, up_pre, wg, wu, wd = items
        arrived_f = arrived.astype(jnp.float32)
        dh = jnp.einsum("psd,fd->psf", arrived_f, wd.astype(jnp.float32))
        g = gate_pre.astype(jnp.float32)
        u = up_pre.astype(jnp.float32)
        sg = jax.nn.sigmoid(g)
        hidden = (g * sg * u).astype(jnp.bfloat16)
        d_up = (dh * g * sg).astype(jnp.bfloat16)
        d_gate = (dh * u * sg * (1.0 + g * (1.0 - sg))).astype(jnp.bfloat16)
        d_slots = jnp.einsum("psf,df->psd", d_gate.astype(jnp.float32), wg.astype(jnp.float32))
        d_slots = d_slots + jnp.einsum("psf,df->psd", d_up.astype(jnp.float32), wu.astype(jnp.float32))
        partial_terms = jnp.einsum("psf,psd->pfd", hidden.astype(jnp.float32), arrived_f).astype(jnp.bfloat16)
        grad = jnp.sum(partial_terms.astype(jnp.float32), axis=0)
        return d_slots.astype(jnp.bfloat16), grad

    d_slots, grad_down = lax.map(one_expert, (slot_rows, gate_rows, up_rows, w_gate, w_up, w_down))
    d_flat = jnp.moveaxis(d_slots, 0, 1).reshape(total_slots, DW)
    d_tokens = d_flat[slot]
    return d_tokens, grad_down
```

```python
import jax
import jax.numpy as jnp
from jax import lax
from jax.experimental import pallas as pl
from jax.experimental.pallas import tpu as pltpu
from jax.sharding import PartitionSpec as P

HALF = 48
RING = 80


def contract_last(left, right):
    return lax.dot_general(
        left, right, (((1,), (1,)), ((), ())), preferred_element_type=jnp.float32
    )


def contract_first(left, right):
    return lax.dot_general(
        left, right, (((0,), (0,)), ((), ())), preferred_element_type=jnp.float32
    )


def shift(block, by, n):
    return lax.ppermute(block, "dp", [(i, (i + by) % n) for i in range(n)])


def stacked_matmul_kernel(*refs):
    left = refs[0]
    blocks = refs[1:-3]
    out, stack, sems = refs[-3:]
    copies, ends, at = [], [], 0
    for i, block in enumerate(blocks):
        copies.append(
            pltpu.make_async_copy(block, stack.at[pl.ds(at, block.shape[0])], sems.at[i])
        )
        at += block.shape[0]
        ends.append(at)
    for copy in copies:
        copy.start()
    done = 0
    for copy, end in zip(copies, ends):
        copy.wait()
        if (end - done >= 256 and end % 128 == 0) or end == at:
            rows = pl.ds(done, end - done)
            out[:, rows] = contract_last(left[...], stack[rows, :]).astype(out.dtype)
            done = end


def stacked_matmul(left, blocks):
    rows, depth = left.shape
    count = sum(block.shape[0] for block in blocks)
    return pl.pallas_call(
        stacked_matmul_kernel,
        out_shape=jax.ShapeDtypeStruct((rows, count), jnp.bfloat16),
        in_specs=[pl.BlockSpec(memory_space=pltpu.VMEM)]
        + [pl.BlockSpec(memory_space=pl.ANY)] * len(blocks),
        out_specs=pl.BlockSpec(memory_space=pltpu.VMEM),
        scratch_shapes=[
            pltpu.VMEM((count, depth), jnp.bfloat16),
            pltpu.SemaphoreType.DMA((len(blocks),)),
        ],
        compiler_params=pltpu.CompilerParams(vmem_limit_bytes=56 * 2**20),
        cost_estimate=pl.CostEstimate(
            flops=2 * rows * depth * count,
            bytes_accessed=2 * depth * (count + rows),
            transcendentals=0,
        ),
    )(left, *blocks)


def per_device(out_grad, gates, expert_ids, saved_gate, saved_up, w_gate, w_up, w_down):
    n_exp = lax.axis_size("expert")
    n_dp = lax.axis_size("dp")
    me = lax.axis_index("dp")
    slots, width_f = saved_gate.shape
    width_d = out_grad.shape[1]
    capacity = slots // n_exp
    rows = w_down.shape[1]
    part = rows // 2
    bf16 = jnp.bfloat16

    pair = jnp.concatenate([w_gate[0], w_up[0]], axis=1)
    down = jnp.concatenate([w_down[0, :part], w_down[0, part:]], axis=1)
    down = jnp.concatenate([down, pair[RING:]])
    deep = -(-down.shape[0] // 8) * 8
    gathered = lax.all_gather(
        jnp.pad(down, ((0, deep - down.shape[0]), (0, 0))), "dp", axis=0, tiled=False
    )
    down = gathered.reshape(n_dp * deep, 2 * width_d)
    rest = gathered[:, part : part + rows - RING].reshape(n_dp * (rows - RING), 2 * width_d)
    own = pair[:RING]

    right, left = shift(own, 1, n_dp), shift(own, -1, n_dp)
    steps = [(right, left)]

    onehot = (expert_ids[:, None] == jnp.arange(n_exp, dtype=jnp.int32)[None, :]).astype(jnp.int32)
    earlier = jnp.cumsum(onehot, axis=0) - onehot
    rank = jnp.sum(earlier * onehot, axis=1)
    target = expert_ids * capacity + rank
    placing = (target[:, None] == jnp.arange(slots, dtype=jnp.int32)[None, :]).astype(bf16)
    scaled = (gates[:, None] * out_grad.astype(jnp.float32)).astype(bf16)
    outgoing = contract_first(placing, scaled).astype(bf16).reshape(n_exp, capacity, width_d)

    unit = jnp.arange(width_f, dtype=jnp.int32)
    side = unit // part % 2

    def spreading(stride):
        at = unit // rows * stride + unit % part
        column = jnp.arange(n_dp * stride, dtype=jnp.int32)[None, :]
        return [((at[:, None] == column) & (side[:, None] == h)).astype(bf16) for h in (0, 1)]

    def spread_out(a, spread):
        return jnp.concatenate(
            [jnp.dot(a, s, preferred_element_type=jnp.float32).astype(bf16) for s in spread]
        )

    def gather_in(a, spread):
        return (contract_last(a[:slots], spread[0]) + contract_last(a[slots:], spread[1])).astype(bf16)

    gate_f = saved_gate.astype(jnp.float32)
    hidden = (gate_f * jax.nn.sigmoid(gate_f) * saved_up.astype(jnp.float32)).astype(bf16)
    right, left, outgoing, hidden = lax.optimization_barrier((right, left, outgoing, hidden))

    right, left = shift(right, 1, n_dp), shift(left, -1, n_dp)
    arrived = lax.all_to_all(outgoing, "expert", split_axis=0, concat_axis=0, tiled=True)
    hidden = spread_out(hidden, spreading(HALF))
    right, left, hidden = lax.optimization_barrier((right, left, hidden))
    steps.append((right, left))

    right, left = shift(right, 1, n_dp), shift(left, -1, n_dp)
    spread = spreading(deep)
    gate_pre = spread_out(saved_gate, spread)
    up_pre = spread_out(saved_up, spread)
    right, left, arrived, gate_pre, up_pre = lax.optimization_barrier(
        (right, left, arrived, gate_pre, up_pre)
    )
    steps.append((right, left))

    right, left = shift(right, 1, n_dp), shift(left, -1, n_dp)
    arrived = arrived.reshape(slots, width_d)
    none = jnp.zeros_like(arrived)
    twice = jnp.concatenate(
        [jnp.concatenate([arrived, none], axis=1), jnp.concatenate([none, arrived], axis=1)]
    )
    right, left, twice = lax.optimization_barrier((right, left, twice))
    steps.append((right, left))

    partial = contract_first(hidden, twice).astype(bf16)
    grad = lax.psum_scatter(partial, "dp", scatter_dimension=0, tiled=True)[:part]
    grad = jnp.concatenate([grad[:, :width_d], grad[:, width_d:]]).astype(jnp.float32)
    right, left = shift(right, 1, n_dp), shift(left, -1, n_dp)
    right, left, down, rest = lax.optimization_barrier((right, left, down, rest))
    steps.append((right, left))

    right, left = shift(right, 1, n_dp), shift(left, -1, n_dp)
    dh = contract_last(twice, down)
    gate_pre = gate_pre.astype(jnp.float32)
    up_pre = up_pre.astype(jnp.float32)
    sigma = jax.nn.sigmoid(gate_pre)
    d_up = (dh * gate_pre * sigma).astype(bf16)
    d_gate = (dh * up_pre * sigma * (1.0 + gate_pre * (1.0 - sigma))).astype(bf16)
    both = jnp.concatenate([gather_in(d_gate, spread), gather_in(d_up, spread)], axis=1)
    right, left, both = lax.optimization_barrier((right, left, both))
    steps.append((right, left))

    def exchange(back):
        back = back.reshape(n_exp, capacity, -1)
        back = lax.all_to_all(back, "expert", split_axis=0, concat_axis=0, tiled=True)
        return back.reshape(slots, -1)

    def result(back, places):
        mine = jnp.dot(placing, back, preferred_element_type=jnp.float32).astype(bf16)
        order = jnp.concatenate(places)[:, None] == jnp.arange(width_d, dtype=jnp.int32)[None, :]
        return jnp.dot(mine, order.astype(bf16), preferred_element_type=jnp.float32)

    def place(offset):
        return (me + offset + n_dp) % n_dp * rows + jnp.arange(RING, dtype=jnp.int32)

    right, left = shift(right, 1, n_dp), shift(left, -1, n_dp)
    extra = jnp.arange(n_dp * (rows - RING), dtype=jnp.int32)
    blocks = [rest, own]
    places = [extra // (rows - RING) * rows + RING + extra % (rows - RING), place(0)]
    for step, pieces in enumerate(steps, 1):
        blocks += pieces
        places += [place(-step), place(step)]
    early = stacked_matmul(both, blocks)
    right, left, early = lax.optimization_barrier((right, left, early))

    cut = RING // 32 * 16 + 16
    ends = [shift(right[:cut], 1, n_dp), shift(left[cut:], -1, n_dp)]
    early = result(exchange(early), places).astype(bf16)
    ends[0], ends[1], early = lax.optimization_barrier((ends[0], ends[1], early))
    late = stacked_matmul(both, [right, left] + ends)
    last = n_dp // 2
    late = result(exchange(late), [place(1 - last), place(last - 1), place(last)])
    d_tokens = (early.astype(jnp.float32) + late).astype(bf16)
    return (d_tokens, grad[None])


def solution(mesh):
    in_specs = (
        P(("dp", "expert"), None),
        P(("dp", "expert")),
        P(("dp", "expert")),
        P(("dp", "expert"), None),
        P(("dp", "expert"), None),
        P("expert", "dp", None),
        P("expert", "dp", None),
        P("expert", "dp", None),
    )
    out_specs = (P(("dp", "expert"), None), P("expert", "dp", None))
    return jax.shard_map(
        per_device, mesh=mesh, in_specs=in_specs, out_specs=out_specs, check_vma=False
    )
```

```python
import jax
import jax.numpy as jnp
from jax import lax
from jax.experimental import pallas as pl
from jax.experimental.pallas import tpu as pltpu
from jax.sharding import PartitionSpec as P

HALF = 48
RING = 80


def contract_last(left, right):
    return lax.dot_general(
        left, right, (((1,), (1,)), ((), ())), preferred_element_type=jnp.float32
    )


def contract_first(left, right):
    return lax.dot_general(
        left, right, (((0,), (0,)), ((), ())), preferred_element_type=jnp.float32
    )


def shift(block, by, n):
    return lax.ppermute(block, "dp", [(i, (i + by) % n) for i in range(n)])


def stacked_matmul_kernel(*refs):
    left = refs[0]
    blocks = refs[1:-3]
    out, stack, sems = refs[-3:]
    copies, ends, at = [], [], 0
    for i, block in enumerate(blocks):
        copies.append(
            pltpu.make_async_copy(block, stack.at[pl.ds(at, block.shape[0])], sems.at[i])
        )
        at += block.shape[0]
        ends.append(at)
    for copy in copies:
        copy.start()
    done = 0
    for copy, end in zip(copies, ends):
        copy.wait()
        if (end - done >= 256 and end % 128 == 0) or end == at:
            rows = pl.ds(done, end - done)
            out[:, rows] = contract_last(left[...], stack[rows, :]).astype(out.dtype)
            done = end


def stacked_matmul(left, blocks):
    rows, depth = left.shape
    count = sum(block.shape[0] for block in blocks)
    return pl.pallas_call(
        stacked_matmul_kernel,
        out_shape=jax.ShapeDtypeStruct((rows, count), jnp.bfloat16),
        in_specs=[pl.BlockSpec(memory_space=pltpu.VMEM)]
        + [pl.BlockSpec(memory_space=pl.ANY)] * len(blocks),
        out_specs=pl.BlockSpec(memory_space=pltpu.VMEM),
        scratch_shapes=[
            pltpu.VMEM((count, depth), jnp.bfloat16),
            pltpu.SemaphoreType.DMA((len(blocks),)),
        ],
        compiler_params=pltpu.CompilerParams(vmem_limit_bytes=56 * 2**20),
        cost_estimate=pl.CostEstimate(
            flops=2 * rows * depth * count,
            bytes_accessed=2 * depth * (count + rows),
            transcendentals=0,
        ),
    )(left, *blocks)


def per_device(out_grad, gates, expert_ids, saved_gate, saved_up, w_gate, w_up, w_down):
    n_exp = lax.axis_size("expert")
    n_dp = lax.axis_size("dp")
    me = lax.axis_index("dp")
    slots, width_f = saved_gate.shape
    width_d = out_grad.shape[1]
    capacity = slots // n_exp
    rows = w_down.shape[1]
    part = rows // 2
    bf16 = jnp.bfloat16

    pair = jnp.concatenate([w_gate[0], w_up[0]], axis=1)
    down = jnp.concatenate([w_down[0, :part], w_down[0, part:]], axis=1)
    down = jnp.concatenate([down, pair[RING:]])
    deep = -(-down.shape[0] // 8) * 8
    gathered = lax.all_gather(
        jnp.pad(down, ((0, deep - down.shape[0]), (0, 0))), "dp", axis=0, tiled=False
    )
    down = gathered.reshape(n_dp * deep, 2 * width_d)
    rest = gathered[:, part : part + rows - RING].reshape(n_dp * (rows - RING), 2 * width_d)
    own = pair[:RING]

    right, left = shift(own, 1, n_dp), shift(own, -1, n_dp)
    steps = [(right, left)]

    onehot = (expert_ids[:, None] == jnp.arange(n_exp, dtype=jnp.int32)[None, :]).astype(jnp.int32)
    earlier = jnp.cumsum(onehot, axis=0) - onehot
    rank = jnp.sum(earlier * onehot, axis=1)
    target = expert_ids * capacity + rank
    placing = (target[:, None] == jnp.arange(slots, dtype=jnp.int32)[None, :]).astype(bf16)
    scaled = (gates[:, None] * out_grad.astype(jnp.float32)).astype(bf16)
    outgoing = contract_first(placing, scaled).astype(bf16).reshape(n_exp, capacity, width_d)

    unit = jnp.arange(width_f, dtype=jnp.int32)
    side = unit // part % 2

    def spreading(stride):
        at = unit // rows * stride + unit % part
        column = jnp.arange(n_dp * stride, dtype=jnp.int32)[None, :]
        return [((at[:, None] == column) & (side[:, None] == h)).astype(bf16) for h in (0, 1)]

    def spread_out(a, spread):
        return jnp.concatenate(
            [jnp.dot(a, s, preferred_element_type=jnp.float32).astype(bf16) for s in spread]
        )

    def gather_in(a, spread):
        return (contract_last(a[:slots], spread[0]) + contract_last(a[slots:], spread[1])).astype(bf16)

    gate_f = saved_gate.astype(jnp.float32)
    hidden = (gate_f * jax.nn.sigmoid(gate_f) * saved_up.astype(jnp.float32)).astype(bf16)
    right, left, hidden = lax.optimization_barrier((right, left, hidden))

    right, left = shift(right, 1, n_dp), shift(left, -1, n_dp)
    arrived = lax.all_to_all(outgoing, "expert", split_axis=0, concat_axis=0, tiled=True)
    hidden = spread_out(hidden, spreading(HALF))
    right, left, hidden = lax.optimization_barrier((right, left, hidden))
    steps.append((right, left))

    right, left = shift(right, 1, n_dp), shift(left, -1, n_dp)
    spread = spreading(deep)
    gate_pre = spread_out(saved_gate, spread)
    up_pre = spread_out(saved_up, spread)
    right, left, arrived, gate_pre, up_pre = lax.optimization_barrier(
        (right, left, arrived, gate_pre, up_pre)
    )
    steps.append((right, left))

    right, left = shift(right, 1, n_dp), shift(left, -1, n_dp)
    arrived = arrived.reshape(slots, width_d)
    none = jnp.zeros_like(arrived)
    twice = jnp.concatenate(
        [jnp.concatenate([arrived, none], axis=1), jnp.concatenate([none, arrived], axis=1)]
    )
    partial = contract_first(hidden, twice).astype(bf16)
    right, left, twice, _ = lax.optimization_barrier((right, left, twice, partial[:8, :128]))
    steps.append((right, left))

    grad = lax.psum_scatter(partial, "dp", scatter_dimension=0, tiled=True)[:part]
    right, left = shift(right, 1, n_dp), shift(left, -1, n_dp)
    right, left, down, rest = lax.optimization_barrier((right, left, down, rest))
    steps.append((right, left))

    right, left = shift(right, 1, n_dp), shift(left, -1, n_dp)
    dh = contract_last(twice, down)
    gate_pre = gate_pre.astype(jnp.float32)
    up_pre = up_pre.astype(jnp.float32)
    sigma = jax.nn.sigmoid(gate_pre)
    d_up = (dh * gate_pre * sigma).astype(bf16)
    d_gate = (dh * up_pre * sigma * (1.0 + gate_pre * (1.0 - sigma))).astype(bf16)
    both = jnp.concatenate([gather_in(d_gate, spread), gather_in(d_up, spread)], axis=1)
    right, left, both = lax.optimization_barrier((right, left, both))
    steps.append((right, left))

    def exchange(back):
        back = back.reshape(n_exp, capacity, -1)
        back = lax.all_to_all(back, "expert", split_axis=0, concat_axis=0, tiled=True)
        return back.reshape(slots, -1)

    def result(back, places):
        mine = jnp.dot(placing, back, preferred_element_type=jnp.float32).astype(bf16)
        order = jnp.concatenate(places)[:, None] == jnp.arange(width_d, dtype=jnp.int32)[None, :]
        return jnp.dot(mine, order.astype(bf16), preferred_element_type=jnp.float32)

    def place(offset):
        return (me + offset + n_dp) % n_dp * rows + jnp.arange(RING, dtype=jnp.int32)

    right, left = shift(right, 1, n_dp), shift(left, -1, n_dp)
    extra = jnp.arange(n_dp * (rows - RING), dtype=jnp.int32)
    blocks = [rest, own]
    places = [extra // (rows - RING) * rows + RING + extra % (rows - RING), place(0)]
    for step, pieces in enumerate(steps, 1):
        blocks += pieces
        places += [place(-step), place(step)]
    early = stacked_matmul(both, blocks)
    early = exchange(early)

    cut = RING // 32 * 16 + 16
    ends = [shift(right[:cut], 1, n_dp), shift(left[cut:], -1, n_dp)]
    late = stacked_matmul(both, [right, left] + ends)
    _, grad, early = lax.optimization_barrier((late, grad, early))
    grad = jnp.concatenate([grad[:, :width_d], grad[:, width_d:]]).astype(jnp.float32)
    early = result(early, places).astype(bf16)
    last = n_dp // 2
    late = result(exchange(late), [place(1 - last), place(last - 1), place(last)])
    d_tokens = (early.astype(jnp.float32) + late).astype(bf16)
    return (d_tokens, grad[None])


def solution(mesh):
    in_specs = (
        P(("dp", "expert"), None),
        P(("dp", "expert")),
        P(("dp", "expert")),
        P(("dp", "expert"), None),
        P(("dp", "expert"), None),
        P("expert", "dp", None),
        P("expert", "dp", None),
        P("expert", "dp", None),
    )
    out_specs = (P(("dp", "expert"), None), P("expert", "dp", None))
    return jax.shard_map(
        per_device, mesh=mesh, in_specs=in_specs, out_specs=out_specs, check_vma=False
    )
```

```python
import jax
import jax.numpy as jnp
from jax import lax
from jax.experimental import pallas as pl
from jax.experimental.pallas import tpu as pltpu
from jax.sharding import PartitionSpec as P

HALF = 48
RING = 64


def contract_last(left, right):
    return lax.dot_general(
        left, right, (((1,), (1,)), ((), ())), preferred_element_type=jnp.float32
    )


def contract_first(left, right):
    return lax.dot_general(
        left, right, (((0,), (0,)), ((), ())), preferred_element_type=jnp.float32
    )


def shift(block, by, n):
    return lax.ppermute(block, "dp", [(i, (i + by) % n) for i in range(n)])


def stacked_matmul_kernel(*refs):
    left = refs[0]
    blocks = refs[1:-3]
    out, stack, sems = refs[-3:]
    copies, ends, at = [], [], 0
    for i, block in enumerate(blocks):
        copies.append(
            pltpu.make_async_copy(block, stack.at[pl.ds(at, block.shape[0])], sems.at[i])
        )
        at += block.shape[0]
        ends.append(at)
    for copy in copies:
        copy.start()
    done = 0
    for copy, end in zip(copies, ends):
        copy.wait()
        if (end - done >= 256 and end % 128 == 0) or end == at:
            rows = pl.ds(done, end - done)
            out[:, rows] = contract_last(left[...], stack[rows, :]).astype(out.dtype)
            done = end


def stacked_matmul(left, blocks):
    rows, depth = left.shape
    count = sum(block.shape[0] for block in blocks)
    return pl.pallas_call(
        stacked_matmul_kernel,
        out_shape=jax.ShapeDtypeStruct((rows, count), jnp.bfloat16),
        in_specs=[pl.BlockSpec(memory_space=pltpu.VMEM)]
        + [pl.BlockSpec(memory_space=pl.ANY)] * len(blocks),
        out_specs=pl.BlockSpec(memory_space=pltpu.VMEM),
        scratch_shapes=[
            pltpu.VMEM((count, depth), jnp.bfloat16),
            pltpu.SemaphoreType.DMA((len(blocks),)),
        ],
        compiler_params=pltpu.CompilerParams(vmem_limit_bytes=56 * 2**20),
        cost_estimate=pl.CostEstimate(
            flops=2 * rows * depth * count,
            bytes_accessed=2 * depth * (count + rows),
            transcendentals=0,
        ),
    )(left, *blocks)


def per_device(out_grad, gates, expert_ids, saved_gate, saved_up, w_gate, w_up, w_down):
    n_exp = lax.axis_size("expert")
    n_dp = lax.axis_size("dp")
    me = lax.axis_index("dp")
    slots, width_f = saved_gate.shape
    width_d = out_grad.shape[1]
    capacity = slots // n_exp
    rows = w_down.shape[1]
    part = rows // 2
    bf16 = jnp.bfloat16

    pair = jnp.concatenate([w_gate[0], w_up[0]], axis=1)
    down = jnp.concatenate([w_down[0, :part], w_down[0, part:]], axis=1)
    down = jnp.concatenate([down, pair[RING:]])
    deep = -(-down.shape[0] // 8) * 8
    gathered = lax.all_gather(
        jnp.pad(down, ((0, deep - down.shape[0]), (0, 0))), "dp", axis=0, tiled=False
    )
    down = gathered.reshape(n_dp * deep, 2 * width_d)
    rest = gathered[:, part : part + rows - RING].reshape(n_dp * (rows - RING), 2 * width_d)
    own = pair[:RING]

    right, left = shift(own, 1, n_dp), shift(own, -1, n_dp)
    steps = [(right, left)]

    onehot = (expert_ids[:, None] == jnp.arange(n_exp, dtype=jnp.int32)[None, :]).astype(jnp.int32)
    earlier = jnp.cumsum(onehot, axis=0) - onehot
    rank = jnp.sum(earlier * onehot, axis=1)
    target = expert_ids * capacity + rank
    placing = (target[:, None] == jnp.arange(slots, dtype=jnp.int32)[None, :]).astype(bf16)
    scaled = (gates[:, None] * out_grad.astype(jnp.float32)).astype(bf16)
    outgoing = contract_first(placing, scaled).astype(bf16).reshape(n_exp, capacity, width_d)

    unit = jnp.arange(width_f, dtype=jnp.int32)
    side = unit // part % 2

    def spreading(stride):
        at = unit // rows * stride + unit % part
        column = jnp.arange(n_dp * stride, dtype=jnp.int32)[None, :]
        return [((at[:, None] == column) & (side[:, None] == h)).astype(bf16) for h in (0, 1)]

    def spread_out(a, spread):
        return jnp.concatenate(
            [jnp.dot(a, s, preferred_element_type=jnp.float32).astype(bf16) for s in spread]
        )

    def gather_in(a, spread):
        return (contract_last(a[:slots], spread[0]) + contract_last(a[slots:], spread[1])).astype(bf16)

    gate_f = saved_gate.astype(jnp.float32)
    hidden = (gate_f * jax.nn.sigmoid(gate_f) * saved_up.astype(jnp.float32)).astype(bf16)
    right, left, hidden = lax.optimization_barrier((right, left, hidden))

    right, left = shift(right, 1, n_dp), shift(left, -1, n_dp)
    arrived = lax.all_to_all(outgoing, "expert", split_axis=0, concat_axis=0, tiled=True)
    hidden = spread_out(hidden, spreading(HALF))
    right, left, hidden = lax.optimization_barrier((right, left, hidden))
    steps.append((right, left))

    right, left = shift(right, 1, n_dp), shift(left, -1, n_dp)
    spread = spreading(deep)
    gate_pre = spread_out(saved_gate, spread)
    up_pre = spread_out(saved_up, spread)
    right, left, arrived, gate_pre, up_pre = lax.optimization_barrier(
        (right, left, arrived, gate_pre, up_pre)
    )
    steps.append((right, left))

    right, left = shift(right, 1, n_dp), shift(left, -1, n_dp)
    arrived = arrived.reshape(slots, width_d)
    none = jnp.zeros_like(arrived)
    twice = jnp.concatenate(
        [jnp.concatenate([arrived, none], axis=1), jnp.concatenate([none, arrived], axis=1)]
    )
    partial = contract_first(hidden, twice).astype(bf16)
    right, left, twice = lax.optimization_barrier((right, left, twice))
    steps.append((right, left))

    grad = lax.psum_scatter(partial, "dp", scatter_dimension=0, tiled=True)[:part]
    right, left = shift(right, 1, n_dp), shift(left, -1, n_dp)
    right, left, down, rest = lax.optimization_barrier((right, left, down, rest))
    steps.append((right, left))

    right, left = shift(right, 1, n_dp), shift(left, -1, n_dp)
    dh = contract_last(twice, down)
    gate_pre = gate_pre.astype(jnp.float32)
    up_pre = up_pre.astype(jnp.float32)
    sigma = jax.nn.sigmoid(gate_pre)
    d_up = (dh * gate_pre * sigma).astype(bf16)
    d_gate = (dh * up_pre * sigma * (1.0 + gate_pre * (1.0 - sigma))).astype(bf16)
    both = jnp.concatenate([gather_in(d_gate, spread), gather_in(d_up, spread)], axis=1)
    right, left, both = lax.optimization_barrier((right, left, both))
    steps.append((right, left))

    def exchange(back):
        back = back.reshape(n_exp, capacity, -1)
        back = lax.all_to_all(back, "expert", split_axis=0, concat_axis=0, tiled=True)
        return back.reshape(slots, -1)

    def result(back, places):
        mine = jnp.dot(placing, back, preferred_element_type=jnp.float32).astype(bf16)
        order = jnp.concatenate(places)[:, None] == jnp.arange(width_d, dtype=jnp.int32)[None, :]
        return jnp.dot(mine, order.astype(bf16), preferred_element_type=jnp.float32)

    def place(offset):
        return (me + offset + n_dp) % n_dp * rows + jnp.arange(RING, dtype=jnp.int32)

    right, left = shift(right, 1, n_dp), shift(left, -1, n_dp)
    extra = jnp.arange(n_dp * (rows - RING), dtype=jnp.int32)
    blocks = [rest, own]
    places = [extra // (rows - RING) * rows + RING + extra % (rows - RING), place(0)]
    for step, pieces in enumerate(steps, 1):
        blocks += pieces
        places += [place(-step), place(step)]
    early = stacked_matmul(both, blocks)
    right, left, early = lax.optimization_barrier((right, left, early))
    early = exchange(early)

    cut = RING // 32 * 16
    ends = [shift(right[:cut], 1, n_dp), shift(left[cut:], -1, n_dp)]
    late = stacked_matmul(both, [right, left] + ends)
    late, early = lax.optimization_barrier((late, early))
    early = result(early, places).astype(bf16)
    last = n_dp // 2
    late = exchange(late)
    grad, late = lax.optimization_barrier((grad, late))
    late = result(late, [place(1 - last), place(last - 1), place(last)])
    d_tokens = (early.astype(jnp.float32) + late).astype(bf16)
    grad = jnp.concatenate([grad[:, :width_d], grad[:, width_d:]]).astype(jnp.float32)
    return (d_tokens, grad[None])


def solution(mesh):
    in_specs = (
        P(("dp", "expert"), None),
        P(("dp", "expert")),
        P(("dp", "expert")),
        P(("dp", "expert"), None),
        P(("dp", "expert"), None),
        P("expert", "dp", None),
        P("expert", "dp", None),
        P("expert", "dp", None),
    )
    out_specs = (P(("dp", "expert"), None), P("expert", "dp", None))
    return jax.shard_map(
        per_device, mesh=mesh, in_specs=in_specs, out_specs=out_specs, check_vma=False
    )
```

```python
import jax
import jax.numpy as jnp
from jax import lax
from jax.experimental import pallas as pl
from jax.experimental.pallas import tpu as pltpu
from jax.sharding import PartitionSpec as P

HALF = 48
RING = 80


def contract_last(left, right):
    return lax.dot_general(
        left, right, (((1,), (1,)), ((), ())), preferred_element_type=jnp.float32
    )


def contract_first(left, right):
    return lax.dot_general(
        left, right, (((0,), (0,)), ((), ())), preferred_element_type=jnp.float32
    )


def shift(block, by, n):
    return lax.ppermute(block, "dp", [(i, (i + by) % n) for i in range(n)])


def stacked_matmul_kernel(*refs):
    left = refs[0]
    blocks = refs[1:-3]
    out, stack, sems = refs[-3:]
    copies, ends, at = [], [], 0
    for i, block in enumerate(blocks):
        copies.append(
            pltpu.make_async_copy(block, stack.at[pl.ds(at, block.shape[0])], sems.at[i])
        )
        at += block.shape[0]
        ends.append(at)
    for copy in copies:
        copy.start()
    done = 0
    for copy, end in zip(copies, ends):
        copy.wait()
        if (end - done >= 256 and end % 128 == 0) or end == at:
            rows = pl.ds(done, end - done)
            out[:, rows] = contract_last(left[...], stack[rows, :]).astype(out.dtype)
            done = end


def stacked_matmul(left, blocks):
    rows, depth = left.shape
    count = sum(block.shape[0] for block in blocks)
    return pl.pallas_call(
        stacked_matmul_kernel,
        out_shape=jax.ShapeDtypeStruct((rows, count), jnp.bfloat16),
        in_specs=[pl.BlockSpec(memory_space=pltpu.VMEM)]
        + [pl.BlockSpec(memory_space=pl.ANY)] * len(blocks),
        out_specs=pl.BlockSpec(memory_space=pltpu.VMEM),
        scratch_shapes=[
            pltpu.VMEM((count, depth), jnp.bfloat16),
            pltpu.SemaphoreType.DMA((len(blocks),)),
        ],
        compiler_params=pltpu.CompilerParams(vmem_limit_bytes=56 * 2**20),
        cost_estimate=pl.CostEstimate(
            flops=2 * rows * depth * count,
            bytes_accessed=2 * depth * (count + rows),
            transcendentals=0,
        ),
    )(left, *blocks)


def per_device(out_grad, gates, expert_ids, saved_gate, saved_up, w_gate, w_up, w_down):
    n_exp = lax.axis_size("expert")
    n_dp = lax.axis_size("dp")
    me = lax.axis_index("dp")
    slots, width_f = saved_gate.shape
    width_d = out_grad.shape[1]
    capacity = slots // n_exp
    rows = w_down.shape[1]
    part = rows // 2
    bf16 = jnp.bfloat16

    pair = jnp.concatenate([w_gate[0], w_up[0]], axis=1)
    down = jnp.concatenate([w_down[0, :part], w_down[0, part:]], axis=1)
    down = jnp.concatenate([down, pair[RING:]])
    deep = -(-down.shape[0] // 8) * 8
    gathered = lax.all_gather(
        jnp.pad(down, ((0, deep - down.shape[0]), (0, 0))), "dp", axis=0, tiled=False
    )
    own = pair[:RING]

    last = n_dp // 2
    right, left = shift(own, 1, n_dp), shift(own, -1, n_dp)
    steps = [(right, left)]

    onehot = (expert_ids[:, None] == jnp.arange(n_exp, dtype=jnp.int32)[None, :]).astype(jnp.int32)
    earlier = jnp.cumsum(onehot, axis=0) - onehot
    rank = jnp.sum(earlier * onehot, axis=1)
    target = expert_ids * capacity + rank
    placing = (target[:, None] == jnp.arange(slots, dtype=jnp.int32)[None, :]).astype(bf16)
    scaled = (gates[:, None] * out_grad.astype(jnp.float32)).astype(bf16)
    outgoing = contract_first(placing, scaled).astype(bf16).reshape(n_exp, capacity, width_d)

    unit = jnp.arange(width_f, dtype=jnp.int32)
    side = unit // part % 2

    def spreading(stride):
        at = unit // rows * stride + unit % part
        column = jnp.arange(n_dp * stride, dtype=jnp.int32)[None, :]
        return [((at[:, None] == column) & (side[:, None] == h)).astype(bf16) for h in (0, 1)]

    def spread_out(a, spread):
        return jnp.concatenate(
            [jnp.dot(a, s, preferred_element_type=jnp.float32).astype(bf16) for s in spread]
        )

    def gather_in(a, spread):
        return (contract_last(a[:slots], spread[0]) + contract_last(a[slots:], spread[1])).astype(bf16)

    gate_f = saved_gate.astype(jnp.float32)
    hidden = (gate_f * jax.nn.sigmoid(gate_f) * saved_up.astype(jnp.float32)).astype(bf16)
    right, left, hidden = lax.optimization_barrier((right, left, hidden))

    right, left = shift(right, 1, n_dp), shift(left, -1, n_dp)
    arrived = lax.all_to_all(outgoing, "expert", split_axis=0, concat_axis=0, tiled=True)
    hidden = spread_out(hidden, spreading(HALF))
    right, left, hidden = lax.optimization_barrier((right, left, hidden))
    steps.append((right, left))

    right, left = shift(right, 1, n_dp), shift(left, -1, n_dp)
    spread = spreading(deep)
    gate_pre = spread_out(saved_gate, spread)
    up_pre = spread_out(saved_up, spread)
    right, left, arrived, gate_pre, up_pre = lax.optimization_barrier(
        (right, left, arrived, gate_pre, up_pre)
    )
    steps.append((right, left))

    right, left = shift(right, 1, n_dp), shift(left, -1, n_dp)
    arrived = arrived.reshape(slots, width_d)
    none = jnp.zeros_like(arrived)
    twice = jnp.concatenate(
        [jnp.concatenate([arrived, none], axis=1), jnp.concatenate([none, arrived], axis=1)]
    )
    partial = contract_first(hidden, twice).astype(bf16)
    right, left, twice, gathered = lax.optimization_barrier((right, left, twice, gathered))
    steps.append((right, left))

    grad = lax.psum_scatter(partial, "dp", scatter_dimension=0, tiled=True)[:part]
    right, left = shift(right, 1, n_dp), shift(left, -1, n_dp)
    dh = contract_last(twice, gathered.reshape(n_dp * deep, 2 * width_d))
    gate_pre = gate_pre.astype(jnp.float32)
    up_pre = up_pre.astype(jnp.float32)
    sigma = jax.nn.sigmoid(gate_pre)
    d_up = (dh * gate_pre * sigma).astype(bf16)
    d_gate = (dh * up_pre * sigma * (1.0 + gate_pre * (1.0 - sigma))).astype(bf16)
    both = jnp.concatenate([gather_in(d_gate, spread), gather_in(d_up, spread)], axis=1)
    right, left, both = lax.optimization_barrier((right, left, both))
    steps.append((right, left))

    def exchange(back):
        back = back.reshape(n_exp, capacity, -1)
        back = lax.all_to_all(back, "expert", split_axis=0, concat_axis=0, tiled=True)
        return back.reshape(slots, -1)

    def result(back, places):
        mine = jnp.dot(placing, back, preferred_element_type=jnp.float32).astype(bf16)
        order = jnp.concatenate(places)[:, None] == jnp.arange(width_d, dtype=jnp.int32)[None, :]
        return jnp.dot(mine, order.astype(bf16), preferred_element_type=jnp.float32)

    def place(offset):
        return (me + offset + n_dp) % n_dp * rows + jnp.arange(RING, dtype=jnp.int32)

    right, left = shift(right, 1, n_dp), shift(left, -1, n_dp)
    rest = gathered[:, part : part + rows - RING].reshape(n_dp * (rows - RING), 2 * width_d)
    extra = jnp.arange(n_dp * (rows - RING), dtype=jnp.int32)
    blocks = [rest, own]
    places = [extra // (rows - RING) * rows + RING + extra % (rows - RING), place(0)]
    for step, pieces in enumerate(steps, 1):
        blocks += pieces
        places += [place(-step), place(step)]
    early = stacked_matmul(both, blocks)
    right, left, early = lax.optimization_barrier((right, left, early))

    pieces = right, left
    right, left = shift(right, 1, n_dp), shift(left, -1, n_dp)
    places += [place(2 - last), place(last - 2)]
    early = exchange(jnp.concatenate([early, stacked_matmul(both, pieces)], axis=1))

    cut = RING // 32 * 16 + 16
    ends = [shift(right[:cut], 1, n_dp), shift(left[cut:], -1, n_dp)]
    late = stacked_matmul(both, [right, left] + ends)
    _, grad, early = lax.optimization_barrier((late, grad, early))
    grad = jnp.concatenate([grad[:, :width_d], grad[:, width_d:]]).astype(jnp.float32)
    early = result(early, places).astype(bf16)
    late = result(exchange(late), [place(1 - last), place(last - 1), place(last)])
    d_tokens = (early.astype(jnp.float32) + late).astype(bf16)
    return (d_tokens, grad[None])


def solution(mesh):
    in_specs = (
        P(("dp", "expert"), None),
        P(("dp", "expert")),
        P(("dp", "expert")),
        P(("dp", "expert"), None),
        P(("dp", "expert"), None),
        P("expert", "dp", None),
        P("expert", "dp", None),
        P("expert", "dp", None),
    )
    out_specs = (P(("dp", "expert"), None), P("expert", "dp", None))
    return jax.shard_map(
        per_device, mesh=mesh, in_specs=in_specs, out_specs=out_specs, check_vma=False
    )
```

```python
import jax
import jax.numpy as jnp
from jax import lax
from jax.experimental import pallas as pl
from jax.experimental.pallas import tpu as pltpu
from jax.sharding import PartitionSpec as P

HALF = 48
RING = 64


def contract_last(left, right):
    return lax.dot_general(
        left, right, (((1,), (1,)), ((), ())), preferred_element_type=jnp.float32
    )


def contract_first(left, right):
    return lax.dot_general(
        left, right, (((0,), (0,)), ((), ())), preferred_element_type=jnp.float32
    )


def shift(block, by, n):
    return lax.ppermute(block, "dp", [(i, (i + by) % n) for i in range(n)])


def stacked_matmul_kernel(*refs):
    left = refs[0]
    blocks = refs[1:-3]
    out, stack, sems = refs[-3:]
    copies, ends, at = [], [], 0
    for i, block in enumerate(blocks):
        copies.append(
            pltpu.make_async_copy(block, stack.at[pl.ds(at, block.shape[0])], sems.at[i])
        )
        at += block.shape[0]
        ends.append(at)
    for copy in copies:
        copy.start()
    done = 0
    for copy, end in zip(copies, ends):
        copy.wait()
        if (end - done >= 256 and end % 128 == 0) or end == at:
            rows = pl.ds(done, end - done)
            out[:, rows] = contract_last(left[...], stack[rows, :]).astype(out.dtype)
            done = end


def stacked_matmul(left, blocks):
    rows, depth = left.shape
    count = sum(block.shape[0] for block in blocks)
    return pl.pallas_call(
        stacked_matmul_kernel,
        out_shape=jax.ShapeDtypeStruct((rows, count), jnp.bfloat16),
        in_specs=[pl.BlockSpec(memory_space=pltpu.VMEM)]
        + [pl.BlockSpec(memory_space=pl.ANY)] * len(blocks),
        out_specs=pl.BlockSpec(memory_space=pltpu.VMEM),
        scratch_shapes=[
            pltpu.VMEM((count, depth), jnp.bfloat16),
            pltpu.SemaphoreType.DMA((len(blocks),)),
        ],
        compiler_params=pltpu.CompilerParams(vmem_limit_bytes=56 * 2**20),
        cost_estimate=pl.CostEstimate(
            flops=2 * rows * depth * count,
            bytes_accessed=2 * depth * (count + rows),
            transcendentals=0,
        ),
    )(left, *blocks)


def per_device(out_grad, gates, expert_ids, saved_gate, saved_up, w_gate, w_up, w_down):
    n_exp = lax.axis_size("expert")
    n_dp = lax.axis_size("dp")
    me = lax.axis_index("dp")
    slots, width_f = saved_gate.shape
    width_d = out_grad.shape[1]
    capacity = slots // n_exp
    rows = w_down.shape[1]
    part = rows // 2
    bf16 = jnp.bfloat16

    pair = jnp.concatenate([w_gate[0], w_up[0]], axis=1)
    down = jnp.concatenate([w_down[0, :part], w_down[0, part:]], axis=1)
    down = jnp.concatenate([down, pair[RING:]])
    deep = -(-down.shape[0] // 8) * 8
    gathered = lax.all_gather(
        jnp.pad(down, ((0, deep - down.shape[0]), (0, 0))), "dp", axis=0, tiled=False
    )
    own = pair[:RING]

    last = n_dp // 2
    right, left = shift(own, 1, n_dp), shift(own, -1, n_dp)
    steps = [(right, left)]

    onehot = (expert_ids[:, None] == jnp.arange(n_exp, dtype=jnp.int32)[None, :]).astype(jnp.int32)
    earlier = jnp.cumsum(onehot, axis=0) - onehot
    rank = jnp.sum(earlier * onehot, axis=1)
    target = expert_ids * capacity + rank
    placing = (target[:, None] == jnp.arange(slots, dtype=jnp.int32)[None, :]).astype(bf16)
    scaled = (gates[:, None] * out_grad.astype(jnp.float32)).astype(bf16)
    outgoing = contract_first(placing, scaled).astype(bf16).reshape(n_exp, capacity, width_d)

    unit = jnp.arange(width_f, dtype=jnp.int32)
    side = unit // part % 2

    def spreading(stride):
        at = unit // rows * stride + unit % part
        column = jnp.arange(n_dp * stride, dtype=jnp.int32)[None, :]
        return [((at[:, None] == column) & (side[:, None] == h)).astype(bf16) for h in (0, 1)]

    def spread_out(a, spread):
        return jnp.concatenate(
            [jnp.dot(a, s, preferred_element_type=jnp.float32).astype(bf16) for s in spread]
        )

    def gather_in(a, spread):
        return (contract_last(a[:slots], spread[0]) + contract_last(a[slots:], spread[1])).astype(bf16)

    gate_f = saved_gate.astype(jnp.float32)
    hidden = (gate_f * jax.nn.sigmoid(gate_f) * saved_up.astype(jnp.float32)).astype(bf16)
    right, left, hidden = lax.optimization_barrier((right, left, hidden))

    right, left = shift(right, 1, n_dp), shift(left, -1, n_dp)
    arrived = lax.all_to_all(outgoing, "expert", split_axis=0, concat_axis=0, tiled=True)
    hidden = spread_out(hidden, spreading(HALF))
    right, left, hidden = lax.optimization_barrier((right, left, hidden))
    steps.append((right, left))

    right, left = shift(right, 1, n_dp), shift(left, -1, n_dp)
    spread = spreading(deep)
    gate_pre = spread_out(saved_gate, spread)
    up_pre = spread_out(saved_up, spread)
    right, left, arrived, gate_pre, up_pre = lax.optimization_barrier(
        (right, left, arrived, gate_pre, up_pre)
    )
    steps.append((right, left))

    right, left = shift(right, 1, n_dp), shift(left, -1, n_dp)
    arrived = arrived.reshape(slots, width_d)
    none = jnp.zeros_like(arrived)
    twice = jnp.concatenate(
        [jnp.concatenate([arrived, none], axis=1), jnp.concatenate([none, arrived], axis=1)]
    )
    partial = contract_first(hidden, twice).astype(bf16)
    right, left, twice = lax.optimization_barrier((right, left, twice))
    steps.append((right, left))

    grad = lax.psum_scatter(partial, "dp", scatter_dimension=0, tiled=True)[:part]
    right, left = shift(right, 1, n_dp), shift(left, -1, n_dp)
    dh = contract_last(twice, gathered.reshape(n_dp * deep, 2 * width_d))
    gate_pre = gate_pre.astype(jnp.float32)
    up_pre = up_pre.astype(jnp.float32)
    sigma = jax.nn.sigmoid(gate_pre)
    d_up = (dh * gate_pre * sigma).astype(bf16)
    d_gate = (dh * up_pre * sigma * (1.0 + gate_pre * (1.0 - sigma))).astype(bf16)
    both = jnp.concatenate([gather_in(d_gate, spread), gather_in(d_up, spread)], axis=1)
    right, left, both = lax.optimization_barrier((right, left, both))
    steps.append((right, left))

    def exchange(back):
        back = back.reshape(n_exp, capacity, -1)
        back = lax.all_to_all(back, "expert", split_axis=0, concat_axis=0, tiled=True)
        return back.reshape(slots, -1)

    def result(back, places):
        mine = jnp.dot(placing, back, preferred_element_type=jnp.float32).astype(bf16)
        order = jnp.concatenate(places)[:, None] == jnp.arange(width_d, dtype=jnp.int32)[None, :]
        return jnp.dot(mine, order.astype(bf16), preferred_element_type=jnp.float32)

    def place(offset):
        return (me + offset + n_dp) % n_dp * rows + jnp.arange(RING, dtype=jnp.int32)

    right, left = shift(right, 1, n_dp), shift(left, -1, n_dp)
    rest = gathered[:, part : part + rows - RING].reshape(n_dp * (rows - RING), 2 * width_d)
    extra = jnp.arange(n_dp * (rows - RING), dtype=jnp.int32)
    blocks = [rest, own]
    places = [extra // (rows - RING) * rows + RING + extra % (rows - RING), place(0)]
    for step, pieces in enumerate(steps, 1):
        blocks += pieces
        places += [place(-step), place(step)]
    early = stacked_matmul(both, blocks)
    right, left, early = lax.optimization_barrier((right, left, early))

    pieces = right, left
    right, left = shift(right, 1, n_dp), shift(left, -1, n_dp)
    places += [place(2 - last), place(last - 2)]
    early = jnp.concatenate([early, stacked_matmul(both, pieces)], axis=1)
    right, left, early = lax.optimization_barrier((right, left, early))
    early = exchange(early)

    cut = RING // 32 * 16
    ends = [shift(right[:cut], 1, n_dp), shift(left[cut:], -1, n_dp)]
    late = stacked_matmul(both, [right, left] + ends)
    late, early = lax.optimization_barrier((late, early))
    early = result(early, places).astype(bf16)
    late = exchange(late)
    grad, late = lax.optimization_barrier((grad, late))
    grad = jnp.concatenate([grad[:, :width_d], grad[:, width_d:]]).astype(jnp.float32)
    late = result(late, [place(1 - last), place(last - 1), place(last)])
    d_tokens = (early.astype(jnp.float32) + late).astype(bf16)
    return (d_tokens, grad[None])


def solution(mesh):
    in_specs = (
        P(("dp", "expert"), None),
        P(("dp", "expert")),
        P(("dp", "expert")),
        P(("dp", "expert"), None),
        P(("dp", "expert"), None),
        P("expert", "dp", None),
        P("expert", "dp", None),
        P("expert", "dp", None),
    )
    out_specs = (P(("dp", "expert"), None), P("expert", "dp", None))
    return jax.shard_map(
        per_device, mesh=mesh, in_specs=in_specs, out_specs=out_specs, check_vma=False
    )
```

```python
import jax
import jax.numpy as jnp
from jax import lax
from jax.experimental import pallas as pl
from jax.experimental.pallas import tpu as pltpu
from jax.sharding import PartitionSpec as P

HALF = 48
RING = 80


def contract_last(left, right):
    return lax.dot_general(
        left, right, (((1,), (1,)), ((), ())), preferred_element_type=jnp.float32
    )


def contract_first(left, right):
    return lax.dot_general(
        left, right, (((0,), (0,)), ((), ())), preferred_element_type=jnp.float32
    )


def shift(block, by, n):
    return lax.ppermute(block, "dp", [(i, (i + by) % n) for i in range(n)])


def stacked_matmul_kernel(*refs):
    left = refs[0]
    blocks = refs[1:-3]
    out, stack, sems = refs[-3:]
    copies, ends, at = [], [], 0
    for i, block in enumerate(blocks):
        copies.append(
            pltpu.make_async_copy(block, stack.at[pl.ds(at, block.shape[0])], sems.at[i])
        )
        at += block.shape[0]
        ends.append(at)
    for copy in copies:
        copy.start()
    done = 0
    for copy, end in zip(copies, ends):
        copy.wait()
        if (end - done >= 256 and end % 128 == 0) or end == at:
            rows = pl.ds(done, end - done)
            out[:, rows] = contract_last(left[...], stack[rows, :]).astype(out.dtype)
            done = end


def stacked_matmul(left, blocks):
    rows, depth = left.shape
    count = sum(block.shape[0] for block in blocks)
    return pl.pallas_call(
        stacked_matmul_kernel,
        out_shape=jax.ShapeDtypeStruct((rows, count), jnp.bfloat16),
        in_specs=[pl.BlockSpec(memory_space=pltpu.VMEM)]
        + [pl.BlockSpec(memory_space=pl.ANY)] * len(blocks),
        out_specs=pl.BlockSpec(memory_space=pltpu.VMEM),
        scratch_shapes=[
            pltpu.VMEM((count, depth), jnp.bfloat16),
            pltpu.SemaphoreType.DMA((len(blocks),)),
        ],
        compiler_params=pltpu.CompilerParams(vmem_limit_bytes=56 * 2**20),
        cost_estimate=pl.CostEstimate(
            flops=2 * rows * depth * count,
            bytes_accessed=2 * depth * (count + rows),
            transcendentals=0,
        ),
    )(left, *blocks)


def per_device(out_grad, gates, expert_ids, saved_gate, saved_up, w_gate, w_up, w_down):
    n_exp = lax.axis_size("expert")
    n_dp = lax.axis_size("dp")
    me = lax.axis_index("dp")
    slots, width_f = saved_gate.shape
    width_d = out_grad.shape[1]
    capacity = slots // n_exp
    rows = w_down.shape[1]
    part = rows // 2
    bf16 = jnp.bfloat16

    pair = jnp.concatenate([w_gate[0], w_up[0]], axis=1)
    down = jnp.concatenate([w_down[0, :part], w_down[0, part:]], axis=1)
    down = jnp.concatenate([down, pair[RING:]])
    deep = -(-down.shape[0] // 8) * 8
    gathered = lax.all_gather(
        jnp.pad(down, ((0, deep - down.shape[0]), (0, 0))), "dp", axis=0, tiled=False
    )
    own = pair[:RING]

    last = n_dp // 2
    right, left = shift(own, 1, n_dp), shift(own, -1, n_dp)
    steps = [(right, left)]

    onehot = (expert_ids[:, None] == jnp.arange(n_exp, dtype=jnp.int32)[None, :]).astype(jnp.int32)
    earlier = jnp.cumsum(onehot, axis=0) - onehot
    rank = jnp.sum(earlier * onehot, axis=1)
    target = expert_ids * capacity + rank
    placing = (target[:, None] == jnp.arange(slots, dtype=jnp.int32)[None, :]).astype(bf16)
    scaled = (gates[:, None] * out_grad.astype(jnp.float32)).astype(bf16)
    outgoing = contract_first(placing, scaled).astype(bf16).reshape(n_exp, capacity, width_d)

    unit = jnp.arange(width_f, dtype=jnp.int32)
    side = unit // part % 2

    def spreading(stride):
        at = unit // rows * stride + unit % part
        column = jnp.arange(n_dp * stride, dtype=jnp.int32)[None, :]
        return [((at[:, None] == column) & (side[:, None] == h)).astype(bf16) for h in (0, 1)]

    def spread_out(a, spread):
        return jnp.concatenate(
            [jnp.dot(a, s, preferred_element_type=jnp.float32).astype(bf16) for s in spread]
        )

    def gather_in(a, spread):
        return (contract_last(a[:slots], spread[0]) + contract_last(a[slots:], spread[1])).astype(bf16)

    gate_f = saved_gate.astype(jnp.float32)
    hidden = (gate_f * jax.nn.sigmoid(gate_f) * saved_up.astype(jnp.float32)).astype(bf16)
    right, left, hidden = lax.optimization_barrier((right, left, hidden))

    right, left = shift(right, 1, n_dp), shift(left, -1, n_dp)
    arrived = lax.all_to_all(outgoing, "expert", split_axis=0, concat_axis=0, tiled=True)
    hidden = spread_out(hidden, spreading(HALF))
    right, left, hidden = lax.optimization_barrier((right, left, hidden))
    steps.append((right, left))

    right, left = shift(right, 1, n_dp), shift(left, -1, n_dp)
    spread = spreading(deep)
    gate_pre = spread_out(saved_gate, spread)
    up_pre = spread_out(saved_up, spread)
    right, left, arrived, gate_pre, up_pre = lax.optimization_barrier(
        (right, left, arrived, gate_pre, up_pre)
    )
    steps.append((right, left))

    right, left = shift(right, 1, n_dp), shift(left, -1, n_dp)
    arrived = arrived.reshape(slots, width_d)
    none = jnp.zeros_like(arrived)
    twice = jnp.concatenate(
        [jnp.concatenate([arrived, none], axis=1), jnp.concatenate([none, arrived], axis=1)]
    )
    partial = contract_first(hidden, twice).astype(bf16)
    right, left, twice, gathered = lax.optimization_barrier((right, left, twice, gathered))
    steps.append((right, left))

    grad = lax.psum_scatter(partial, "dp", scatter_dimension=0, tiled=True)[:part]
    right, left = shift(right, 1, n_dp), shift(left, -1, n_dp)
    dh = contract_last(twice, gathered.reshape(n_dp * deep, 2 * width_d))
    gate_pre = gate_pre.astype(jnp.float32)
    up_pre = up_pre.astype(jnp.float32)
    sigma = jax.nn.sigmoid(gate_pre)
    d_up = (dh * gate_pre * sigma).astype(bf16)
    d_gate = (dh * up_pre * sigma * (1.0 + gate_pre * (1.0 - sigma))).astype(bf16)
    both = jnp.concatenate([gather_in(d_gate, spread), gather_in(d_up, spread)], axis=1)
    right, left, both = lax.optimization_barrier((right, left, both))
    steps.append((right, left))

    def exchange(back):
        back = back.reshape(n_exp, capacity, -1)
        back = lax.all_to_all(back, "expert", split_axis=0, concat_axis=0, tiled=True)
        return back.reshape(slots, -1)

    def result(back, places):
        mine = jnp.dot(placing, back, preferred_element_type=jnp.float32).astype(bf16)
        order = jnp.concatenate(places)[:, None] == jnp.arange(width_d, dtype=jnp.int32)[None, :]
        return jnp.dot(mine, order.astype(bf16), preferred_element_type=jnp.float32)

    def place(offset):
        return (me + offset + n_dp) % n_dp * rows + jnp.arange(RING, dtype=jnp.int32)

    right, left = shift(right, 1, n_dp), shift(left, -1, n_dp)
    rest = gathered[:, part : part + rows - RING].reshape(n_dp * (rows - RING), 2 * width_d)
    extra = jnp.arange(n_dp * (rows - RING), dtype=jnp.int32)
    blocks = [rest, own]
    places = [extra // (rows - RING) * rows + RING + extra % (rows - RING), place(0)]
    for step, pieces in enumerate(steps, 1):
        blocks += pieces
        places += [place(-step), place(step)]
    early = stacked_matmul(both, blocks)
    right, left, early = lax.optimization_barrier((right, left, early))

    pieces = right, left
    right, left = shift(right, 1, n_dp), shift(left, -1, n_dp)
    places += [place(2 - last), place(last - 2)]
    early = exchange(jnp.concatenate([early, stacked_matmul(both, pieces)], axis=1))

    cut = RING // 32 * 16 + 16
    ends = [shift(right[:cut], 1, n_dp), shift(left[cut:], -1, n_dp)]
    late = [stacked_matmul(both, [right, left]), stacked_matmul(both, ends)]
    late = jnp.concatenate(late, axis=1)
    _, grad, early = lax.optimization_barrier((late, grad, early))
    grad = jnp.concatenate([grad[:, :width_d], grad[:, width_d:]]).astype(jnp.float32)
    early = result(early, places).astype(bf16)
    late = result(exchange(late), [place(1 - last), place(last - 1), place(last)])
    d_tokens = (early.astype(jnp.float32) + late).astype(bf16)
    return (d_tokens, grad[None])


def solution(mesh):
    in_specs = (
        P(("dp", "expert"), None),
        P(("dp", "expert")),
        P(("dp", "expert")),
        P(("dp", "expert"), None),
        P(("dp", "expert"), None),
        P("expert", "dp", None),
        P("expert", "dp", None),
        P("expert", "dp", None),
    )
    out_specs = (P(("dp", "expert"), None), P("expert", "dp", None))
    return jax.shard_map(
        per_device, mesh=mesh, in_specs=in_specs, out_specs=out_specs, check_vma=False
    )
```
